32 devices in a mesh: replica: 8 (over z, core), shard: 4 (over y, x).
Axes of the slice: x: 2, y: 2, z: 4, core: 2. Of those that a mesh axis runs over, the one named last changes fastest.
Arguments:
- tokens: bfloat16 [32768, 640], P(('replica', 'shard')), may hold values from -6 to 6
- positions: int32 [32768], P(('replica', 'shard')), may hold values from 0 to 1023, as said below
- cotangent: bfloat16 [32768, 640], P(('replica', 'shard')), may hold values from -6 to 6
- q_weight: bfloat16 [640, 1024], P('shard'), may hold values from -0.25 to 0.25
- k_weight: bfloat16 [640, 256], P('shard'), may hold values from -0.25 to 0.25
- v_weight: bfloat16 [640, 256], P('shard'), may hold values from -0.25 to 0.25
- o_weight: bfloat16 [1024, 640], P('shard'), may hold values from -0.1875 to 0.1875
- gate_weight: bfloat16 [640, 2048], P('shard'), may hold values from -0.25 to 0.25
- up_weight: bfloat16 [640, 2048], P('shard'), may hold values from -0.25 to 0.25
- down_weight: bfloat16 [2048, 640], P('shard'), may hold values from -0.125 to 0.125
- attn_gain: bfloat16 [640], P('shard'), may hold values from 0.099609375 to 1.8984375
- query_gain: bfloat16 [256], P('shard'), may hold values from 0.099609375 to 1.8984375
- key_gain: bfloat16 [256], P('shard'), may hold values from 0.099609375 to 1.8984375
- post_attn_gain: bfloat16 [640], P('shard'), may hold values from 0.099609375 to 1.8984375
- pre_ffn_gain: bfloat16 [640], P('shard'), may hold values from 0.099609375 to 1.8984375
- post_ffn_gain: bfloat16 [640], P('shard'), may hold values from 0.099609375 to 1.8984375
Outputs:
- mixed: bfloat16 [32768, 640], P(('replica', 'shard'))
- tokens_grad: float32 [32768, 640], P(('replica', 'shard'))
- q_weight_grad: float32 [640, 1024], P('shard')
- k_weight_grad: float32 [640, 256], P('shard')
- v_weight_grad: float32 [640, 256], P('shard')
- o_weight_grad: float32 [1024, 640], P('shard')
- gate_weight_grad: float32 [640, 2048], P('shard')
- up_weight_grad: float32 [640, 2048], P('shard')
- down_weight_grad: float32 [2048, 640], P('shard')
- attn_gain_grad: float32 [640], P('shard')
- query_gain_grad: float32 [256], P('shard')
- key_gain_grad: float32 [256], P('shard')
- post_attn_gain_grad: float32 [640], P('shard')
- pre_ffn_gain_grad: float32 [640], P('shard')
- post_ffn_gain_grad: float32 [640], P('shard')
The draws below stay inside these ranges and needn't reach their ends.
Inputs may be any that keep to these rules, and one draw needn't show every extreme that they name: `positions`: each aligned block of 1024 tokens holds one to three documents laid end to end; a token's position counts from the start of its document, which never lies before its block's start; in some block one document fills the whole block.
All inputs are finite; a program needn't handle non-finite values.
Results may differ from the reference program's by a relative error of at most 0.015.
Values may be sent and summed in bfloat16 or wider, within the bound.
A program may use at most 192 MiB of HBM per device.

```python
import jax
import jax.numpy as jnp
from jax import lax

D = 640
FF = 2048
HEAD = 256
QHEADS = 4
WINDOW = 512
TOK_DEV = 1024
TOKENS = 32768


def draw_positions(key, part):
    key = jax.random.fold_in(key, 11)
    bound_key, count_key, row_key = jax.random.split(key, 3)
    sequences = TOKENS // TOK_DEV
    bounds = jax.random.randint(bound_key, (sequences, 2), 1, TOK_DEV)
    counts = jax.random.randint(count_key, (sequences,), 0, 3)
    whole_row = jax.random.randint(row_key, (), 0, sequences)
    counts = jnp.where(jnp.arange(sequences) == whole_row, 0, counts)
    index = jnp.arange(TOK_DEV)[None, :]
    first_start = jnp.where((counts[:, None] >= 1) & (bounds[:, 0:1] <= index), bounds[:, 0:1], 0)
    second_start = jnp.where((counts[:, None] >= 2) & (bounds[:, 1:2] <= index), bounds[:, 1:2], 0)
    return (index - jnp.maximum(first_start, second_start)).reshape(-1).astype(jnp.int32)


def draw_tokens(key, part):
    key = jax.random.fold_in(key, 5)
    return jax.random.truncated_normal(key, -6.0, 6.0, (TOKENS, D), jnp.float32).astype(jnp.bfloat16)


def draw_cotangent(key, part):
    key = jax.random.fold_in(key, 7)
    return jax.random.truncated_normal(key, -6.0, 6.0, (TOKENS, D), jnp.float32).astype(jnp.bfloat16)


def level_of(stream_key, extent, shards, low, largest):
    factor_of, own = 1.0, jax.random.fold_in(stream_key, 6)
    for dim, shards_of in shards:
        draws = jnp.exp(jax.random.uniform(jax.random.fold_in(own, dim), (shards_of,), jnp.float32, low / len(shards), largest / len(shards)))
        factor_of = factor_of * jnp.repeat(draws, extent[dim] // shards_of).reshape([-1 if axis == dim else 1 for axis in range(len(extent))])
    return factor_of


def gaussian(own_key, extent, deviation, limit, cuts=(), kind=jnp.bfloat16):
    entries = jax.random.normal(own_key, extent, jnp.float32) * deviation
    if len(cuts) > 0:
        entries = level_of(own_key, extent, cuts, -0.22, 0.18) * entries
    return jnp.clip(entries, min=-limit, max=limit).astype(kind)


def setup_inputs(seed: int = 0) -> dict:
    seeds = jax.random.split(jax.random.key(seed), 17)
    tokens = draw_tokens(jax.random.fold_in(seeds[16], 71), 0)
    positions = draw_positions(jax.random.fold_in(seeds[16], 71), 0)
    cotangent = draw_cotangent(jax.random.fold_in(seeds[16], 71), 0)
    q_weight = gaussian(seeds[3], (D, QHEADS * HEAD), D ** -0.5, 0.25, ((0, 4),))
    k_weight = gaussian(seeds[4], (D, HEAD), D ** -0.5, 0.25, ((0, 4),))
    v_weight = gaussian(seeds[5], (D, HEAD), D ** -0.5, 0.25, ((0, 4),))
    o_weight = gaussian(seeds[6], (QHEADS * HEAD, D), (QHEADS * HEAD) ** -0.5, 0.1875, ((0, 4),))
    gate_weight = gaussian(seeds[7], (D, FF), D ** -0.5, 0.25, ((0, 4),))
    up_weight = gaussian(seeds[8], (D, FF), D ** -0.5, 0.25, ((0, 4),))
    down_weight = gaussian(seeds[9], (FF, D), FF ** -0.5, 0.125, ((0, 4),))
    attn_gain = jnp.clip(1.0 + 0.18 * jax.random.normal(seeds[10], (D,), jnp.float32), 0.099609375, 1.8984375).astype(jnp.bfloat16)
    query_gain = jnp.clip(1.0 + 0.18 * jax.random.normal(seeds[11], (HEAD,), jnp.float32), 0.099609375, 1.8984375).astype(jnp.bfloat16)
    key_gain = jnp.clip(1.0 + 0.18 * jax.random.normal(seeds[12], (HEAD,), jnp.float32), 0.099609375, 1.8984375).astype(jnp.bfloat16)
    post_attn_gain = jnp.clip(1.0 + 0.18 * jax.random.normal(seeds[13], (D,), jnp.float32), 0.099609375, 1.8984375).astype(jnp.bfloat16)
    pre_ffn_gain = jnp.clip(1.0 + 0.18 * jax.random.normal(seeds[14], (D,), jnp.float32), 0.099609375, 1.8984375).astype(jnp.bfloat16)
    post_ffn_gain = jnp.clip(1.0 + 0.18 * jax.random.normal(seeds[15], (D,), jnp.float32), 0.099609375, 1.8984375).astype(jnp.bfloat16)
    return {"tokens": tokens, "positions": positions, "cotangent": cotangent, "q_weight": q_weight, "k_weight": k_weight, "v_weight": v_weight, "o_weight": o_weight, "gate_weight": gate_weight, "up_weight": up_weight, "down_weight": down_weight, "attn_gain": attn_gain, "query_gain": query_gain, "key_gain": key_gain, "post_attn_gain": post_attn_gain, "pre_ffn_gain": pre_ffn_gain, "post_ffn_gain": post_ffn_gain}


@jax.custom_vjp
def low(v):
    return lax.optimization_barrier(v.astype(jnp.bfloat16)).astype(jnp.float32)

@jax.custom_vjp
def low_back(v):
    return v

def low_keep(v):
    return (low(v), None)

def low_pass(kept, grad):
    return (grad,)

def back_keep(v):
    return (v, None)

def back_low(kept, grad):
    return (low(grad),)
low.defvjp(low_keep, low_pass)
low_back.defvjp(back_keep, back_low)
EPSILON = 1e-06
PRECISE = lax.Precision.HIGHEST

def rms_scale(values, scale_gain):
    return values * lax.rsqrt(lax.optimization_barrier(jnp.mean(values * values, axis=-1, keepdims=True)) + EPSILON) * scale_gain

def rotary_angles(positions, head_width):
    indices = jnp.arange(head_width // 2).astype(jnp.float32)
    frequency = 10000.0 ** (-2.0 * indices / head_width)
    return positions.astype(jnp.float32)[:, None] * frequency[None, :]

def rotate(values, angles):
    half_width = values.shape[-1] // 2
    cosine = jnp.cos(angles)[:, None, :]
    sine_part = jnp.sin(angles)[:, None, :]
    front_half = values[..., :half_width]
    back_half = values[..., half_width:]
    return jnp.concatenate([front_half * cosine - back_half * sine_part, back_half * cosine + front_half * sine_part], axis=-1)

def visible_keys(start, query_pos, window):
    row_index = start + jnp.arange(window, dtype=jnp.int32)
    col_index = start - window + jnp.arange(2 * window, dtype=jnp.int32)
    distance = row_index[:, None] - col_index[None, :]
    return (distance >= 0) & (distance < window) & (distance <= query_pos[:, None])

def window_view(rows_in, blocks):
    padded = jnp.concatenate([jnp.zeros((WINDOW, rows_in.shape[1]), rows_in.dtype), rows_in], axis=0)
    padded = padded.reshape(blocks + 1, WINDOW, rows_in.shape[1])
    return jnp.concatenate([padded[:-1], padded[1:]], axis=1)

def attend_block(block_item):
    queries, key_rows, value_rows, query_pos, start = block_item
    scores = low_back(jnp.einsum('qhd,kd->hqk', queries, key_rows, precision=PRECISE))
    scores = jnp.where(visible_keys(start, query_pos, WINDOW)[None], scores, -1e+30)
    highest = lax.optimization_barrier(jnp.max(scores, axis=-1, keepdims=True))
    raised = jnp.exp(scores - highest)
    shares = low(raised / lax.optimization_barrier(jnp.sum(raised, axis=-1, keepdims=True)))
    return jnp.einsum('hqk,kd->qhd', shares, value_rows, precision=PRECISE)

def layer(inputs, positions, q_weight, k_weight, v_weight, o_weight, gate_weight, up_weight, down_weight, attn_gain, query_gain, key_gain, post_attn_gain, pre_ffn_gain, post_ffn_gain):
    length = inputs.shape[0]
    blocks = length // WINDOW
    normed = low(rms_scale(inputs, attn_gain))
    query_raw = low_back(jnp.dot(normed, q_weight, precision=PRECISE)).reshape(length, QHEADS, HEAD)
    key_raw = low_back(jnp.dot(normed, k_weight, precision=PRECISE)).reshape(length, 1, HEAD)
    values = low(low_back(jnp.dot(normed, v_weight, precision=PRECISE)))
    angles = rotary_angles(positions, HEAD)
    queries = low(rotate(rms_scale(query_raw, query_gain), angles) * HEAD ** (-0.5))
    key_rows = low(rotate(rms_scale(key_raw, key_gain), angles))[:, 0, :]
    starts = jnp.arange(blocks, dtype=jnp.int32) * WINDOW
    attended = lax.map(jax.checkpoint(attend_block), (queries.reshape(blocks, WINDOW, QHEADS, HEAD), window_view(key_rows, blocks), window_view(values, blocks), positions.reshape(blocks, WINDOW), starts))
    attended = low(low_back(attended.reshape(length, QHEADS * HEAD)))
    branch = low_back(jnp.dot(attended, o_weight, precision=PRECISE))
    middle = inputs + rms_scale(branch, post_attn_gain)
    inner = low(rms_scale(middle, pre_ffn_gain))
    gate = low_back(jnp.dot(inner, gate_weight, precision=PRECISE))
    upward = low_back(jnp.dot(inner, up_weight, precision=PRECISE))
    hidden = low(jax.nn.gelu(gate, approximate=True) * upward)
    ffn_out = low_back(jnp.dot(hidden, down_weight, precision=PRECISE))
    return middle + rms_scale(ffn_out, post_ffn_gain)

def reference(tokens, positions, cotangent, q_weight, k_weight, v_weight, o_weight, gate_weight, up_weight, down_weight, attn_gain, query_gain, key_gain, post_attn_gain, pre_ffn_gain, post_ffn_gain):
    params = tuple((member.astype(jnp.float32) for member in (q_weight, k_weight, v_weight, o_weight, gate_weight, up_weight, down_weight, attn_gain, query_gain, key_gain, post_attn_gain, pre_ffn_gain, post_ffn_gain)))
    sequences = tokens.shape[0] // TOK_DEV
    width = tokens.shape[1]
    inputs = tokens.astype(jnp.float32).reshape(sequences, TOK_DEV, width)
    upstream = cotangent.astype(jnp.float32).reshape(sequences, TOK_DEV, width)
    places = positions.reshape(sequences, TOK_DEV)

    def one_sequence(totals, seq_item):
        seq_inputs, seq_places, seq_upstream = seq_item

        def forward(arg_inputs, *arg_params):
            return layer(arg_inputs, seq_places, *arg_params)
        result, pullback = jax.vjp(forward, seq_inputs, *params)
        gradients = pullback(seq_upstream)
        summed = tuple((before + after for before, after in zip(totals, gradients[1:])))
        return (summed, (result.astype(jnp.bfloat16), gradients[0]))
    zeros = tuple((jnp.zeros(member.shape, jnp.float32) for member in params))
    totals, (outputs, input_grads) = lax.scan(one_sequence, zeros, (inputs, places, upstream))
    return (outputs.reshape(sequences * TOK_DEV, width), input_grads.reshape(sequences * TOK_DEV, width), totals[0], totals[1], totals[2], totals[3], totals[4], totals[5], totals[6], totals[7], totals[8], totals[9], totals[10], totals[11], totals[12])
```

```python
import jax
import jax.numpy as jnp
from jax import lax
from jax.experimental import pallas as pl
from jax.experimental.pallas import tpu as pltpu
from jax.sharding import PartitionSpec as P

HEAD = 256
WINDOW = 512


EPSILON = 1e-06


def rms_scale(values, scale_gain):
    return (
        values * lax.rsqrt(jnp.mean(values * values, axis=-1, keepdims=True) + EPSILON) * scale_gain
    )


def rotary_angles(positions, head_width):
    indices = jnp.arange(head_width // 2).astype(jnp.float32)
    frequency = 10000.0 ** (-2.0 * indices / head_width)
    return positions.astype(jnp.float32)[:, None] * frequency[None, :]


def visible_keys(start, first, query_pos):
    shape = (WINDOW, start + WINDOW - first)
    row_index = start + lax.broadcasted_iota(jnp.int32, shape, 0)
    col_index = first + lax.broadcasted_iota(jnp.int32, shape, 1)
    distance = row_index - col_index
    return (distance >= 0) & (distance < WINDOW) & (distance <= query_pos)


def kernel_dot(left, right, dims):
    return lax.dot_general(left, right, (dims, ((), ())), preferred_element_type=jnp.float32)


def forward_kernel(query_ref, key_ref, value_ref, place_ref, out_ref, total_ref):
    for start in range(0, query_ref.shape[0], WINDOW):
        first = max(0, start - WINDOW)
        own = pl.ds(start, WINDOW)
        span = pl.ds(first, start + WINDOW - first)
        scores = kernel_dot(query_ref[own, :], key_ref[span, :], ((1,), (1,)))
        seen = visible_keys(start, first, place_ref[own, :])
        scores = jnp.where(seen, scores, -1e30)
        highest = jnp.max(scores, axis=-1, keepdims=True)
        raised = jnp.exp(scores - highest)
        summed = jnp.sum(raised, axis=-1, keepdims=True)
        shares = (raised / summed).astype(jnp.bfloat16)
        out_ref[own, :] = kernel_dot(shares, value_ref[span, :], ((1,), (0,))).astype(
            jnp.bfloat16
        )
        total_ref[0, own, :] = highest + jnp.log(summed)


def backward_kernel(
    query_ref,
    key_ref,
    value_ref,
    place_ref,
    total_ref,
    out_grad_ref,
    query_grad_ref,
    key_grad_ref,
    value_grad_ref,
):
    @pl.when(pl.program_id(0) == 0)
    def _():
        key_grad_ref[...] = jnp.zeros_like(key_grad_ref)
        value_grad_ref[...] = jnp.zeros_like(value_grad_ref)

    for start in range(0, query_ref.shape[0], WINDOW):
        first = max(0, start - WINDOW)
        own = pl.ds(start, WINDOW)
        span = pl.ds(first, start + WINDOW - first)
        queries = query_ref[own, :]
        out_grad = out_grad_ref[own, :]
        key_rows = key_ref[span, :]
        scores = kernel_dot(queries, key_rows, ((1,), (1,)))
        seen = visible_keys(start, first, place_ref[own, :])
        shares = jnp.where(seen, jnp.exp(scores - total_ref[0, own, :]), 0.0)
        share_grad = kernel_dot(out_grad, value_ref[span, :], ((1,), (1,)))
        spread = jnp.sum(shares * share_grad, axis=-1, keepdims=True)
        scores_low = (shares * (share_grad - spread)).astype(jnp.bfloat16)
        query_grad_ref[own, :] = kernel_dot(scores_low, key_rows, ((1,), (0,)))
        key_grad_ref[span, :] += kernel_dot(scores_low, queries, ((0,), (0,)))
        value_grad_ref[span, :] += kernel_dot(shares.astype(jnp.bfloat16), out_grad, ((0,), (0,)))


def attention_specs(length):
    by_head = pl.BlockSpec((length, HEAD), lambda h: (0, h))
    shared = pl.BlockSpec((length, HEAD), lambda h: (0, 0))
    place = pl.BlockSpec((length, 1), lambda h: (0, 0))
    total = pl.BlockSpec((1, length, 1), lambda h: (h, 0, 0))
    return (by_head, shared, place, total)


def attention_forward(queries, key_rows, values, positions):
    length, columns = queries.shape
    heads = columns // HEAD
    by_head, shared, place, total = attention_specs(length)
    return pl.pallas_call(
        forward_kernel,
        grid=(heads,),
        in_specs=[by_head, shared, shared, place],
        out_specs=[by_head, total],
        out_shape=[
            jax.ShapeDtypeStruct((length, columns), jnp.bfloat16),
            jax.ShapeDtypeStruct((heads, length, 1), jnp.float32),
        ],
        compiler_params=pltpu.CompilerParams(vmem_limit_bytes=40 * 2**20),
        cost_estimate=pl.CostEstimate(
            flops=6 * length * WINDOW * columns,
            bytes_accessed=6 * length * columns,
            transcendentals=2 * length * WINDOW * heads,
        ),
        name="attention_forward",
    )(queries, key_rows, values, positions[:, None])


def attention_backward(queries, key_rows, values, positions, totals, out_grad):
    length, columns = queries.shape
    heads = columns // HEAD
    by_head, shared, place, total = attention_specs(length)
    return pl.pallas_call(
        backward_kernel,
        grid=(heads,),
        in_specs=[by_head, shared, shared, place, total, by_head],
        out_specs=[by_head, shared, shared],
        out_shape=[
            jax.ShapeDtypeStruct((length, columns), jnp.float32),
            jax.ShapeDtypeStruct((length, HEAD), jnp.float32),
            jax.ShapeDtypeStruct((length, HEAD), jnp.float32),
        ],
        compiler_params=pltpu.CompilerParams(vmem_limit_bytes=40 * 2**20),
        cost_estimate=pl.CostEstimate(
            flops=15 * length * WINDOW * columns,
            bytes_accessed=12 * length * columns,
            transcendentals=2 * length * WINDOW * heads,
        ),
        name="attention_backward",
    )(queries, key_rows, values, positions[:, None], totals, out_grad)


def gelu_product(gate, upward):
    return jax.nn.gelu(gate, approximate=True) * upward


def rope_pair(values, cosine, sine_part):
    half_width = values.shape[-1] // 2
    front_half = values[..., :half_width]
    back_half = values[..., half_width:]
    return jnp.concatenate(
        [front_half * cosine - back_half * sine_part, back_half * cosine + front_half * sine_part],
        axis=-1,
    )


def swap_cores(member):
    return lax.ppermute(member, "core", [(0, 1), (1, 0)])


def in_core_order(mine, other, core, axis):
    first = jnp.where(core == 0, mine, other)
    second = jnp.where(core == 0, other, mine)
    return jnp.stack([first, second], axis=axis)


def halve_over_owners(member, shard, owners, low_first):
    bits = owners.bit_length() - 1
    pieces = member.reshape((2,) * bits + member.shape[1:])
    left = list(range(bits - 1, -1, -1))
    while left:
        place = len(left) - 1 if low_first else 0
        bit = left.pop(place)
        mine = (shard >> bit) & 1
        sent = lax.dynamic_index_in_dim(pieces, 1 - mine, place, keepdims=False)
        kept = lax.dynamic_index_in_dim(pieces, mine, place, keepdims=False)
        pairs = [(device, device ^ (1 << bit)) for device in range(owners)]
        pieces = kept + lax.ppermute(sent, "shard", pairs)
    return pieces


def reduce_pair(other, mine, shard, owners, low_first):
    paired = mine + swap_cores(other)
    piece = halve_over_owners(paired, shard, owners, low_first)
    return lax.psum(piece, "z")


def body(
    tokens,
    positions,
    cotangent,
    q_weight,
    k_weight,
    v_weight,
    o_weight,
    gate_weight,
    up_weight,
    down_weight,
    attn_gain,
    query_gain,
    key_gain,
    post_attn_gain,
    pre_ffn_gain,
    post_ffn_gain,
):
    core = lax.axis_index("core")
    shard = lax.axis_index("shard")
    owners = lax.axis_size("shard")
    f32 = jnp.float32
    low = jnp.bfloat16
    width = tokens.shape[1]
    length = tokens.shape[0]

    def dot(left, right, dims):
        return lax.dot_general(left, right, (dims, ((), ())), preferred_element_type=f32)

    def gather(half):
        mine = lax.all_gather(half, "shard", axis=0, tiled=False)
        return mine, swap_cores(mine)

    gains = (attn_gain, query_gain, key_gain, post_attn_gain, pre_ffn_gain, post_ffn_gain)
    gain_sizes = [member.shape[0] for member in gains]
    gain_line = jnp.concatenate(gains)
    qkv_weight = jnp.concatenate([q_weight, k_weight, v_weight], axis=1)
    rows, columns = qkv_weight.shape
    gain_rows = -(-gain_line.shape[0] // columns)
    pad_rows = -(-gain_rows // 16) * 16
    gain_block = jnp.pad(gain_line, (0, pad_rows * columns - gain_line.shape[0]))
    gain_block = gain_block.reshape(pad_rows, columns)
    qkv_half = lax.dynamic_index_in_dim(
        qkv_weight.reshape(2, rows // 2, columns), core, 0, keepdims=False
    )
    qkv_mine, qkv_other = gather(jnp.concatenate([qkv_half, gain_block], axis=0))
    gain_all = qkv_mine[:, rows // 2 : rows // 2 + gain_rows].reshape(owners, -1)
    split_gains = []
    offset = 0
    for size in gain_sizes:
        split_gains.append(gain_all[:, offset : offset + size].reshape(-1).astype(f32))
        offset += size
    gain_attn, gain_query, gain_key, gain_post_attn, gain_pre_ffn, gain_post_ffn = split_gains
    qkv_full = in_core_order(
        qkv_mine[:, : rows // 2], qkv_other[:, : rows // 2], core, 1
    ).reshape(owners * rows, columns)

    o_rows = o_weight.shape[0]
    o_half = lax.dynamic_index_in_dim(
        o_weight.reshape(2, o_rows // 2, width), core, 0, keepdims=False
    )
    o_mine, o_other = gather(o_half)
    o_full = in_core_order(o_mine, o_other, core, 1).reshape(owners * o_rows, width)

    unit_half = down_weight.shape[0] // 2

    def unit_columns(member):
        shaped = member.reshape(member.shape[0], owners, 2, unit_half)
        return lax.dynamic_index_in_dim(shaped, core, 2, keepdims=False).reshape(
            member.shape[0], owners * unit_half
        )

    def flat_rows(pair):
        return tuple(member.reshape(-1, member.shape[-1]) for member in pair)

    gate_pair = flat_rows(gather(unit_columns(gate_weight)))
    up_pair = flat_rows(gather(unit_columns(up_weight)))
    down_pair = flat_rows(
        gather(
            lax.dynamic_index_in_dim(
                down_weight.reshape(2, unit_half, width), core, 0, keepdims=False
            )
        )
    )

    window = WINDOW
    blocks = length // window
    inputs = tokens.astype(f32)
    angles = rotary_angles(positions, HEAD)
    cosine = jnp.cos(angles)
    sine_part = jnp.sin(angles)
    normed_f, pull_attn_norm = jax.vjp(rms_scale, inputs, gain_attn)
    normed = normed_f.astype(low)
    q_cols = q_weight.shape[1]
    heads = q_cols // HEAD
    qkv_raw = dot(normed, qkv_full, ((1,), (0,)))
    values = qkv_raw[:, q_cols + HEAD :].astype(low)

    def prepare(raw_rows, scale_gain, factor):
        return rope_pair(rms_scale(raw_rows, scale_gain), cosine, sine_part) * factor

    def prepare_queries(raw_rows, scale_gain):
        return [
            prepare(raw_rows[:, h * HEAD : (h + 1) * HEAD], scale_gain, HEAD ** (-0.5))
            for h in range(heads)
        ]

    queries_f, pull_query = jax.vjp(prepare_queries, qkv_raw[:, :q_cols], gain_query)
    key_f, pull_key = jax.vjp(
        lambda raw_rows, scale_gain: prepare(raw_rows, scale_gain, 1.0),
        qkv_raw[:, q_cols : q_cols + HEAD],
        gain_key,
    )
    queries = jnp.concatenate([member.astype(low) for member in queries_f], axis=1)
    key_rows = key_f.astype(low)
    attended, log_totals = attention_forward(queries, key_rows, values, positions)
    branch = dot(attended, o_full, ((1,), (0,)))
    post_attn_f, pull_post_attn = jax.vjp(rms_scale, branch, gain_post_attn)
    middle = inputs + post_attn_f
    inner_f, pull_pre_ffn = jax.vjp(rms_scale, middle, gain_pre_ffn)
    inner = inner_f.astype(low)
    gates = [dot(inner, member, ((1,), (0,))) for member in gate_pair]
    ups = [dot(inner, member, ((1,), (0,))) for member in up_pair]
    hiddens, pulls = [], []
    for gate, upward in zip(gates, ups):
        hidden_f, pull_glu = jax.vjp(gelu_product, gate, upward)
        hiddens.append(hidden_f.astype(low))
        pulls.append(pull_glu)
    ffn_out = dot(hiddens[0], down_pair[0], ((1,), (0,))) + dot(
        hiddens[1], down_pair[1], ((1,), (0,))
    )
    post_ffn_f, pull_post_ffn = jax.vjp(rms_scale, ffn_out, gain_post_ffn)
    mixed = (middle + post_ffn_f).astype(low)
    upstream = cotangent.astype(f32)
    ffn_grad, post_ffn_gain_grad = pull_post_ffn(upstream)
    ffn_low = ffn_grad.astype(low)

    down_other = dot(hiddens[1], ffn_low, ((0,), (0,))).reshape(owners, unit_half, width)
    down_mine = dot(hiddens[0], ffn_low, ((0,), (0,))).reshape(owners, unit_half, width)
    ffn_low, down_other, down_mine = lax.optimization_barrier((ffn_low, down_other, down_mine))
    down_sum = reduce_pair(down_other, down_mine, shard, owners, False)
    gate_lows, up_lows = [], []
    for pull_glu, down_half in zip(pulls, down_pair):
        hidden_grad = dot(ffn_low, down_half, ((1,), (1,)))
        gate_grad, up_grad = pull_glu(hidden_grad)
        gate_lows.append(gate_grad.astype(low))
        up_lows.append(up_grad.astype(low))
    owner_rows = gate_weight.shape[0]
    gate_other = dot(inner, gate_lows[1], ((0,), (0,))).reshape(owners, owner_rows, -1)
    gate_mine = dot(inner, gate_lows[0], ((0,), (0,))).reshape(owners, owner_rows, -1)
    up_other = dot(inner, up_lows[1], ((0,), (0,))).reshape(owners, owner_rows, -1)
    up_mine = dot(inner, up_lows[0], ((0,), (0,))).reshape(owners, owner_rows, -1)
    gate_lows[0], gate_other, gate_mine, up_other, up_mine = lax.optimization_barrier(
        (gate_lows[0], gate_other, gate_mine, up_other, up_mine)
    )
    gate_sum = reduce_pair(gate_other, gate_mine, shard, owners, True)
    up_sum = reduce_pair(up_other, up_mine, shard, owners, False)
    inner_grad = (
        dot(gate_lows[0], gate_pair[0], ((1,), (1,)))
        + dot(gate_lows[1], gate_pair[1], ((1,), (1,)))
        + dot(up_lows[0], up_pair[0], ((1,), (1,)))
        + dot(up_lows[1], up_pair[1], ((1,), (1,)))
    )
    middle_part, pre_ffn_gain_grad = pull_pre_ffn(inner_grad)
    middle_grad = upstream + middle_part
    branch_grad, post_attn_gain_grad = pull_post_attn(middle_grad)
    branch_low = branch_grad.astype(low)
    attended_parts = attended.reshape(length, owners, 2, o_rows // 2)

    def o_part(which):
        rows_of = lax.dynamic_index_in_dim(attended_parts, which, 2, keepdims=False)
        return dot(rows_of.reshape(length, -1), branch_low, ((0,), (0,))).reshape(
            owners, o_rows // 2, width
        )

    o_other, o_mine = o_part(1 - core), o_part(core)
    branch_low, o_other, o_mine = lax.optimization_barrier((branch_low, o_other, o_mine))
    o_sum = reduce_pair(o_other, o_mine, shard, owners, True)
    attended_grad = dot(branch_low, o_full, ((1,), (1,))).astype(low)
    queries_grad, keys_grad, value_grad = attention_backward(
        queries, key_rows, values, positions, log_totals, attended_grad
    )
    value_low = value_grad.astype(low)
    query_raw_grad, query_gain_grad = pull_query(
        [queries_grad[:, h * HEAD : (h + 1) * HEAD] for h in range(heads)]
    )
    key_raw_grad, key_gain_grad = pull_key(keys_grad)
    qkv_low = jnp.concatenate(
        [query_raw_grad.astype(low), key_raw_grad.astype(low), value_low], axis=1
    )
    half_columns = columns // 2

    def qkv_part(which):
        picked = lax.dynamic_slice_in_dim(qkv_low, which * half_columns, half_columns, 1)
        return dot(normed, picked, ((0,), (0,))).reshape(owners, rows, half_columns)

    qkv_other, qkv_mine = qkv_part(1 - core), qkv_part(core)
    qkv_low, qkv_other, qkv_mine = lax.optimization_barrier((qkv_low, qkv_other, qkv_mine))
    qkv_sum = reduce_pair(qkv_other, qkv_mine, shard, owners, False)
    normed_grad = dot(qkv_low, qkv_full, ((1,), (1,)))
    input_part, attn_gain_grad = pull_attn_norm(normed_grad)
    tokens_grad = middle_grad + input_part
    gain_grads = jnp.concatenate(
        [
            attn_gain_grad,
            query_gain_grad,
            key_gain_grad,
            post_attn_gain_grad,
            pre_ffn_gain_grad,
            post_ffn_gain_grad,
        ]
    )
    gain_sum = lax.psum(gain_grads, ("z", "core", "shard"))
    gain_outs = []
    offset = 0
    for size in gain_sizes:
        gain_outs.append(lax.dynamic_slice_in_dim(gain_sum, offset + shard * size, size, 0))
        offset += size * owners

    def finish(member, axis):
        return in_core_order(member, swap_cores(member), core, axis)

    down_out = finish(down_sum, 0).reshape(2 * unit_half, width)
    gate_out = finish(gate_sum.reshape(owner_rows, owners, unit_half), 2)
    up_out = finish(up_sum.reshape(owner_rows, owners, unit_half), 2)
    o_out = finish(o_sum, 0).reshape(o_rows, width)
    qkv_out = finish(qkv_sum, 1).reshape(rows, columns)
    return (
        mixed,
        tokens_grad,
        qkv_out[:, :q_cols],
        qkv_out[:, q_cols : q_cols + HEAD],
        qkv_out[:, q_cols + HEAD :],
        o_out,
        gate_out.reshape(owner_rows, -1),
        up_out.reshape(owner_rows, -1),
        down_out,
        *gain_outs,
    )


def solution(mesh):
    replicas = mesh.shape["replica"]
    owners = mesh.shape["shard"]
    split = jax.sharding.Mesh(
        mesh.devices.reshape(replicas // 2, 2, owners), ("z", "core", "shard")
    )
    every = ("z", "core", "shard")
    weights = [P("shard", None)] * 7
    gains = [P("shard")] * 6
    return jax.shard_map(
        body,
        mesh=split,
        in_specs=(P(every, None), P(every), P(every, None), *weights, *gains),
        out_specs=(P(every, None), P(every, None), *weights, *gains),
        check_vma=False,
    )
```
